128 devices in a mesh: fsdp: 16 (over y_hi, z, core), tp: 8 (over x, y_lo).
Axes of the slice: x: 4, y: 4 (y_hi: 2, y_lo: 2; y = y_hi * 2 + y_lo), z: 4, core: 2. Of those that a mesh axis runs over, the one named last changes fastest.
Arguments:
- normed: bfloat16 [2, 256, 16384], P(None, None, 'fsdp'), may hold values from -6 to 6
- resident_gate_matrix: bfloat16 [16384, 26624], P('fsdp', 'tp'), may hold values from -0.046875 to 0.046875
- resident_up_matrix: bfloat16 [16384, 26624], P('fsdp', 'tp'), may hold values from -0.046875 to 0.046875
- resident_down_matrix: bfloat16 [26624, 16384], P('tp', 'fsdp'), may hold values from -0.0390625 to 0.0390625
- gate_input_factor: bfloat16 [16, 16384], P(None, ('fsdp', 'tp')), may hold values from -0.046875 to 0.046875
- up_input_factor: bfloat16 [16, 16384], P(None, ('fsdp', 'tp')), may hold values from -0.046875 to 0.046875
- gate_output_factor: bfloat16 [26624, 16], P(('tp', 'fsdp')), may hold values from -0.29882812 to 0.29882812
- up_output_factor: bfloat16 [26624, 16], P(('tp', 'fsdp')), may hold values from -0.29882812 to 0.29882812
- down_input_factor: bfloat16 [16, 26624], P(None, ('tp', 'fsdp')), may hold values from -0.0390625 to 0.0390625
- down_output_factor: bfloat16 [16384, 16], P(('fsdp', 'tp')), may hold values from -0.29882812 to 0.29882812
Outputs:
- mixed: bfloat16 [2, 256, 16384], P(None, 'tp', 'fsdp')
The draws below stay inside these ranges and needn't reach their ends.
All inputs are finite; a program needn't handle non-finite values.
Results may differ from the reference program's by a relative error of at most 0.007.
Values may be sent and summed in bfloat16 or wider, within the bound.
No kernel may reach another device: no remote copies, remote signals or barrier semaphores. Data moves between devices by JAX's collectives and lax.ppermute only.
A program may use at most 128 MiB of HBM per device.

```python
import jax
import jax.numpy as jnp

MODEL_WIDTH = 16384
HIDDEN_WINDOW = 26624
UPDATE_RANK = 16
STEPS = 2
ROWS = 256


def steps_of(own_key, dims, pieces, least, high):
    def one(axis_at, blocks):
        draws = jax.random.uniform(jax.random.fold_in(jax.random.fold_in(own_key, 6), axis_at), (blocks,), jnp.float32, least / len(pieces), high / len(pieces))
        return jnp.repeat(jnp.exp(draws), dims[axis_at] // blocks).reshape((-1,) + (1,) * (len(dims) - axis_at - 1))

    gain = one(*pieces[0])
    for cut in pieces[1:]:
        gain = gain * one(*cut)
    return gain


def noise(own_key, extent, spread, bound, shards=(), held_as=jnp.bfloat16):
    result = jax.random.normal(own_key, extent, jnp.float32) * spread
    if len(shards) > 0:
        result = steps_of(own_key, extent, shards, -0.22, 0.18) * result
    return jnp.clip(result, min=-bound, max=bound).astype(held_as)


def setup_inputs(seed: int = 0) -> dict:
    arg_keys = jax.random.split(jax.random.key(seed), 11)
    return {
        "normed": noise(arg_keys[0], (STEPS, ROWS, MODEL_WIDTH), 1.0, 6.0, ((2, 16),)),
        "resident_gate_matrix": noise(arg_keys[1], (MODEL_WIDTH, HIDDEN_WINDOW), MODEL_WIDTH ** -0.5, 0.046875, ((0, 16), (1, 8))),
        "resident_up_matrix": noise(arg_keys[2], (MODEL_WIDTH, HIDDEN_WINDOW), MODEL_WIDTH ** -0.5, 0.046875, ((0, 16), (1, 8))),
        "resident_down_matrix": noise(arg_keys[3], (HIDDEN_WINDOW, MODEL_WIDTH), HIDDEN_WINDOW ** -0.5, 0.0390625, ((0, 8), (1, 16))),
        "gate_input_factor": noise(arg_keys[4], (UPDATE_RANK, MODEL_WIDTH), MODEL_WIDTH ** -0.5, 0.046875, ((1, 128),)),
        "up_input_factor": noise(arg_keys[5], (UPDATE_RANK, MODEL_WIDTH), MODEL_WIDTH ** -0.5, 0.046875, ((1, 128),)),
        "gate_output_factor": noise(arg_keys[6], (HIDDEN_WINDOW, UPDATE_RANK), 0.05, 0.29882812, ((0, 128),)),
        "up_output_factor": noise(arg_keys[7], (HIDDEN_WINDOW, UPDATE_RANK), 0.05, 0.29882812, ((0, 128),)),
        "down_input_factor": noise(arg_keys[8], (UPDATE_RANK, HIDDEN_WINDOW), HIDDEN_WINDOW ** -0.5, 0.0390625, ((1, 128),)),
        "down_output_factor": noise(arg_keys[9], (MODEL_WIDTH, UPDATE_RANK), 0.05, 0.29882812, ((0, 128),)),
    }


adapter_scale = 2.0


def merge_weight_block(resident_matrix, rank_cols, rank_rows):
    block_parts = []
    weight_block = resident_matrix.shape[0] // 8
    for block_index in range(8):
        lowered_program = block_index * weight_block
        cols_part = rank_cols[:, lowered_program:lowered_program + weight_block]
        adapter_update = jnp.dot(cols_part.T, rank_rows.T, preferred_element_type=jnp.float32)
        block_parts.append((resident_matrix[lowered_program:lowered_program + weight_block].astype(jnp.float32) + adapter_scale * adapter_update).astype(jnp.bfloat16))
    return jnp.concatenate(block_parts, 0)


def reference(normed, resident_gate_matrix, resident_up_matrix, resident_down_matrix, gate_input_factor, up_input_factor, gate_output_factor, up_output_factor, down_input_factor, down_output_factor):
    refreshed_gate_matrix = merge_weight_block(resident_gate_matrix, gate_input_factor, gate_output_factor)
    refreshed_up_matrix = merge_weight_block(resident_up_matrix, up_input_factor, up_output_factor)
    refreshed_down_matrix = merge_weight_block(resident_down_matrix, down_input_factor, down_output_factor)
    outputs = []
    for number in range(STEPS):
        states = normed[number]
        gate_sum = jnp.dot(states, refreshed_gate_matrix, preferred_element_type=jnp.float32)
        up_sum = jnp.dot(states, refreshed_up_matrix, preferred_element_type=jnp.float32)
        hidden = (jax.nn.silu(gate_sum) * up_sum).astype(jnp.bfloat16)
        outputs.append(jnp.dot(hidden, refreshed_down_matrix, preferred_element_type=jnp.float32).astype(jnp.bfloat16))
    return jnp.stack(outputs, 0)
```

```python
import functools

import jax
import jax.numpy as jnp
from jax import lax
from jax.experimental import pallas as pl
from jax.experimental.pallas import tpu as pltpu
from jax.sharding import Mesh
from jax.sharding import PartitionSpec as P

adapter_scale = 2.0
f32 = jnp.float32
bf16 = jnp.bfloat16
FSDP = ("yh", "z", "c")
TP = ("x", "yl")
RANK = 16
VMEM_LIMIT = 48 * 1024 * 1024


def pair_bits(core):
    return 1 + 2 * core, 3 - 2 * core


def fsdp_owner(r):
    yh, z, c = lax.axis_index("yh"), lax.axis_index("z"), lax.axis_index("c")
    cc = c ^ ((r >> 3) & 1)
    a, b = pair_bits(cc)
    zz = z ^ (((r >> 2) & 1) * a) ^ ((r & 1) * b)
    yy = yh ^ ((r >> 1) & 1)
    return (yy * 4 + zz) * 2 + cc


def tp_owner(q):
    x, yl, c = lax.axis_index("x"), lax.axis_index("yl"), lax.axis_index("c")
    a, b = pair_bits(c)
    xx = x ^ (((q >> 2) & 1) * a) ^ (((q >> 1) & 1) * b)
    return xx * 2 + (yl ^ (q & 1))


def swap(axis, value):
    return lax.ppermute(value, axis, [(0, 1), (1, 0)])


def ring_pair(axis, first, value):
    axes = ("z", "c") if axis == "z" else ("c", "x")

    def index(place, core):
        return place * 2 + core if axis == "z" else core * 4 + place

    moves = []
    for place in range(4):
        for core in range(2):
            step = pair_bits(core)[0 if first else 1]
            moves.append((index(place, core), index(place ^ step, core)))
    return lax.ppermute(value, axes, moves)


def xor_pair(axis, step, value):
    return lax.ppermute(value, axis, [(i, i ^ step) for i in range(4)])


def in_vmem(body, name, out_shape, *args, scratch=()):
    whole = pl.BlockSpec(memory_space=pltpu.VMEM)
    outs = tuple(jax.ShapeDtypeStruct(shape, dtype) for shape, dtype in out_shape)
    moved = sum(a.size * a.dtype.itemsize for a in (*args, *outs))
    return pl.pallas_call(
        body,
        in_specs=[whole] * len(args),
        out_specs=[whole] * len(outs),
        out_shape=outs,
        scratch_shapes=scratch,
        compiler_params=pltpu.CompilerParams(vmem_limit_bytes=VMEM_LIMIT),
        cost_estimate=pl.CostEstimate(flops=moved, bytes_accessed=moved, transcendentals=0),
        name=name,
    )(*args)


def rows_at(block, size):
    return pl.ds(pl.multiple_of(block * size, 16), size)


def other_core_body(size, gate_ref, up_ref, send_ref):
    for r in range(8):
        theirs = rows_at(fsdp_owner(8 + r), size)
        send_ref[2 * r * size : (2 * r + 1) * size] = gate_ref[theirs, :]
        send_ref[(2 * r + 1) * size : (2 * r + 2) * size] = up_ref[theirs, :]


def core_sum_body(size, gate_ref, up_ref, recv_ref, rank_ref, rank_recv_ref, keep_ref, send_ref):
    for r in range(8):
        mine = rows_at(fsdp_owner(r), size)
        for i, part_ref in enumerate((gate_ref, up_ref)):
            at = (2 * r + i) * size
            total = part_ref[mine, :].astype(f32) + recv_ref[at : at + size].astype(f32)
            if r < 4:
                keep_ref[at : at + size] = total
            else:
                send_ref[at - 8 * size : at - 7 * size] = total.astype(bf16)
    rank = rank_ref[...] + rank_recv_ref[...]
    keep_ref[8 * size :] = rank
    send_ref[8 * size :] = rank.astype(bf16)


def halve_body(tail, keep_ref, recv_ref, kept_ref, send_ref):
    half = kept_ref.shape[0] - tail
    kept_ref[:half] = keep_ref[:half] + recv_ref[:half].astype(f32)
    send_ref[:half] = (keep_ref[half : 2 * half] + recv_ref[half : 2 * half].astype(f32)).astype(bf16)
    if tail:
        total = keep_ref[2 * half :] + recv_ref[2 * half :].astype(f32)
        kept_ref[half:] = total
        send_ref[half:] = total.astype(bf16)


def halve(keep, recv, tail):
    half = (keep.shape[0] - tail) // 2 + tail
    shape = (half, keep.shape[1])
    return in_vmem(functools.partial(halve_body, tail), "halve", [(shape, f32), (shape, bf16)], keep, recv)


def hidden_body(keep_ref, recv_ref, gate_factor_ref, up_factor_ref, down_factor_ref, out_ref):
    size = gate_factor_ref.shape[0]
    total = keep_ref[...] + recv_ref[...].astype(f32)
    rank = total[2 * size :].astype(bf16)
    sums = []
    for i, factor_ref in enumerate((gate_factor_ref, up_factor_ref)):
        term = jnp.dot(factor_ref[...], rank[RANK * i : RANK * i + RANK], preferred_element_type=f32)
        sums.append(total[i * size : (i + 1) * size] + adapter_scale * term)
    gate, up = sums
    hidden = (gate / (1.0 + jnp.exp(-gate)) * up).astype(bf16)
    out_ref[:size] = hidden
    out_ref[size:] = jnp.dot(down_factor_ref[...], hidden, preferred_element_type=f32).astype(bf16)


def join_body(tail, mine_ref, theirs_ref, out_ref):
    size = mine_ref.shape[0] - tail
    out_ref[:size] = mine_ref[:size]
    out_ref[size : 2 * size] = theirs_ref[:size]
    out_ref[2 * size :] = (mine_ref[size:].astype(f32) + theirs_ref[size:].astype(f32)).astype(bf16)


def join(mine, theirs):
    size = mine.shape[0] - RANK
    shape = (2 * size + RANK, mine.shape[1])
    return in_vmem(functools.partial(join_body, RANK), "join", [(shape, bf16)], mine, theirs)[0]


def spread_body(mine_ref, theirs_ref, out_ref, rank_ref):
    size = (mine_ref.shape[0] - RANK) // 8
    for r in range(16):
        from_ref = theirs_ref if r >> 3 else mine_ref
        at = (r & 7) * size
        out_ref[rows_at(fsdp_owner(r), size), :] = from_ref[at : at + size]
    rank_ref[...] = (mine_ref[8 * size :].astype(f32) + theirs_ref[8 * size :].astype(f32)).astype(bf16)


def tp_order_body(part_ref, rank_ref, factor_ref, keep_ref, send_ref, total_ref):
    size = part_ref.shape[0] // 8
    total_ref[...] = part_ref[...] + adapter_scale * lax.dot_general(
        rank_ref[...], factor_ref[...], (((0,), (0,)), ((), ())), preferred_element_type=f32
    )
    for q in range(8):
        block = total_ref[rows_at(tp_owner(q), size), :]
        if q < 4:
            keep_ref[q * size : (q + 1) * size] = block
        else:
            send_ref[(q - 4) * size : (q - 3) * size] = block.astype(bf16)


def last_body(keep_ref, recv_ref, out_ref):
    out_ref[...] = (keep_ref[...] + recv_ref[...].astype(f32)).astype(bf16)


def after(value, earlier):
    return lax.optimization_barrier((value, earlier))[0]


def double(pack, swapped, high):
    return jnp.where(high == 0, jnp.concatenate([pack, swapped], 0), jnp.concatenate([swapped, pack], 0))


def per_device(
    normed,
    resident_gate_matrix,
    resident_up_matrix,
    resident_down_matrix,
    gate_input_factor,
    up_input_factor,
    gate_output_factor,
    up_output_factor,
    down_input_factor,
    down_output_factor,
):
    x, yl = lax.axis_index("x"), lax.axis_index("yl")
    steps, rows, depth = normed.shape
    units = resident_gate_matrix.shape[1]
    size = units // 16

    wide = jnp.concatenate([gate_input_factor, up_input_factor, down_output_factor.T], 0)[None]
    wide = double(wide, swap("yl", wide), yl)
    wide = double(wide, xor_pair("x", 1, wide), x & 1)
    wide = double(wide, xor_pair("x", 3, wide), x >> 1)
    wide = wide.transpose(1, 0, 2).reshape(wide.shape[1], -1)
    rank = lax.dot_general(
        wide[: 2 * RANK], normed.reshape(steps * rows, depth), (((1,), (1,)), ((), ())), preferred_element_type=f32
    )
    rank_recv = swap("c", rank)

    parts = []
    for s in range(steps):
        gate, up = (
            lax.dot_general(w, normed[s], (((0,), (1,)), ((), ())), preferred_element_type=f32).astype(bf16)
            for w in (resident_gate_matrix, resident_up_matrix)
        )
        (send,) = in_vmem(
            functools.partial(other_core_body, size), "other_core", [((units, rows), bf16)], gate, up
        )
        parts.append((gate, up, swap("c", send)))
    to_near = []
    for s in range(steps):
        shape = (8 * size + 2 * RANK, rows)
        to_near.append(
            in_vmem(
                functools.partial(core_sum_body, size),
                "core_sum",
                [(shape, f32), (shape, bf16)],
                *parts[s],
                rank[:, s * rows : (s + 1) * rows],
                rank_recv[:, s * rows : (s + 1) * rows],
            )
        )
    outputs = []
    earlier = None
    for s in range(steps):
        keep, send = to_near[s]
        if earlier is not None:
            send = after(send, earlier)
        earlier = ring_pair("z", True, send)
        keep, send = halve(keep, earlier, 2 * RANK)
        keep, send = halve(keep, swap("yh", send), 2 * RANK)
        recv = ring_pair("z", False, send)
        (hidden,) = in_vmem(
            hidden_body,
            "hidden",
            [((size + RANK, rows), bf16)],
            keep,
            recv,
            gate_output_factor,
            up_output_factor,
            down_input_factor,
        )
        hidden = join(hidden, ring_pair("z", False, hidden))
        hidden = join(hidden, swap("yh", hidden))
        hidden = join(hidden, ring_pair("z", True, hidden))
        hidden, rank_down = in_vmem(
            spread_body, "spread", [((units, rows), bf16), ((RANK, rows), bf16)], hidden, swap("c", hidden)
        )
        part = lax.dot_general(
            hidden, resident_down_matrix, (((0,), (0,)), ((), ())), preferred_element_type=f32
        )
        half = (rows // 2, part.shape[1])
        keep, send = in_vmem(
            tp_order_body,
            "tp_order",
            [(half, f32), (half, bf16)],
            part,
            rank_down,
            wide[2 * RANK :],
            scratch=[pltpu.VMEM(part.shape, f32)],
        )
        keep, send = halve(keep, ring_pair("x", True, send), 0)
        keep, send = halve(keep, ring_pair("x", False, send), 0)
        outputs.append(in_vmem(last_body, "last", [(keep.shape, bf16)], keep, swap("yl", send))[0])
    return jnp.stack(outputs, 0)


def solution(mesh):
    fine = Mesh(mesh.devices.reshape(2, 4, 2, 4, 2), FSDP + TP)
    fsdp, tp = FSDP, TP
    in_specs = (
        P(None, None, fsdp),
        P(fsdp, tp),
        P(fsdp, tp),
        P(tp, fsdp),
        P(None, fsdp + tp),
        P(None, fsdp + tp),
        P(tp + fsdp, None),
        P(tp + fsdp, None),
        P(None, tp + fsdp),
        P(fsdp + tp, None),
    )
    out_specs = P(None, tp, fsdp)
    return jax.shard_map(
        per_device, mesh=fine, in_specs=in_specs, out_specs=out_specs, check_vma=False
    )
```

```python
import functools

import jax
import jax.numpy as jnp
from jax import lax
from jax.experimental import pallas as pl
from jax.experimental.pallas import tpu as pltpu
from jax.sharding import Mesh
from jax.sharding import PartitionSpec as P

adapter_scale = 2.0
f32 = jnp.float32
bf16 = jnp.bfloat16
FSDP = ("yh", "z", "c")
TP = ("x", "yl")
RANK = 16
VMEM_LIMIT = 16 * 1024 * 1024
ORDER = (0, 1, 0, 1, 0, 1, 0, 1, 0, 0, 0, 1, 0, 1, 0, 1, 0, 1)


def pair_bits(core):
    return 1 + 2 * core, 3 - 2 * core


def fsdp_owner(r, y_first):
    yh, z, c = lax.axis_index("yh"), lax.axis_index("z"), lax.axis_index("c")
    core, (first_z, second_z, y) = (r >> 3) & 1, ((r >> 2) & 1, (r >> 1) & 1, r & 1)
    if y_first:
        y, first_z, second_z = first_z, second_z, y
    cc = c ^ core
    a, b = pair_bits(cc)
    zz = z ^ (first_z * a) ^ (second_z * b)
    return ((yh ^ y) * 4 + zz) * 2 + cc


def tp_owner(q):
    x, yl, c = lax.axis_index("x"), lax.axis_index("yl"), lax.axis_index("c")
    a, b = pair_bits(c)
    xx = x ^ (((q >> 2) & 1) * a) ^ (((q >> 1) & 1) * b)
    return xx * 2 + (yl ^ (q & 1))


def swap(axis, value):
    return lax.ppermute(value, axis, [(0, 1), (1, 0)])


def ring_pair(axis, first, value):
    axes = ("z", "c") if axis == "z" else ("c", "x")

    def index(place, core):
        return place * 2 + core if axis == "z" else core * 4 + place

    moves = []
    for place in range(4):
        for core in range(2):
            step = pair_bits(core)[0 if first else 1]
            moves.append((index(place, core), index(place ^ step, core)))
    return lax.ppermute(value, axes, moves)


def exchange(axes, value):
    return lax.all_to_all(value, axes, split_axis=0, concat_axis=0)


def in_vmem(body, name, out_shape, *args, scratch=()):
    whole = pl.BlockSpec(memory_space=pltpu.VMEM)
    outs = tuple(jax.ShapeDtypeStruct(shape, dtype) for shape, dtype in out_shape)
    moved = sum(a.size * a.dtype.itemsize for a in (*args, *outs))
    return pl.pallas_call(
        body,
        in_specs=[whole] * len(args),
        out_specs=[whole] * len(outs),
        out_shape=outs,
        scratch_shapes=scratch,
        compiler_params=pltpu.CompilerParams(vmem_limit_bytes=VMEM_LIMIT),
        cost_estimate=pl.CostEstimate(flops=moved, bytes_accessed=moved, transcendentals=0),
        name=name,
    )(*args)


def rows_at(block, size):
    return pl.ds(pl.multiple_of(block * size, 16), size)


def other_core_body(size, step, gate_ref, up_ref, send_ref):
    lanes = pl.ds(step * send_ref.shape[1], send_ref.shape[1])
    for r in range(8):
        theirs = rows_at(fsdp_owner(8 + r, step), size)
        send_ref[2 * r * size : (2 * r + 1) * size] = gate_ref[theirs, lanes]
        send_ref[(2 * r + 1) * size : (2 * r + 2) * size] = up_ref[theirs, lanes]


def core_sum_body(size, step, gate_ref, up_ref, recv_ref, rank_ref, rank_recv_ref, keep_ref, send_ref):
    lanes = pl.ds(step * recv_ref.shape[1], recv_ref.shape[1])
    for r in range(8):
        mine = rows_at(fsdp_owner(r, step), size)
        for i, part_ref in enumerate((gate_ref, up_ref)):
            at = (2 * r + i) * size
            total = part_ref[mine, lanes].astype(f32) + recv_ref[at : at + size].astype(f32)
            if r < 4:
                keep_ref[at : at + size] = total
            else:
                send_ref[at - 8 * size : at - 7 * size] = total.astype(bf16)
    rank = rank_ref[:, lanes] + rank_recv_ref[:, lanes]
    keep_ref[8 * size :] = rank
    send_ref[8 * size :] = rank.astype(bf16)


def halve_body(tail, keep_ref, recv_ref, kept_ref, send_ref):
    half = kept_ref.shape[0] - tail
    kept_ref[:half] = keep_ref[:half] + recv_ref[:half].astype(f32)
    send_ref[:half] = (keep_ref[half : 2 * half] + recv_ref[half : 2 * half].astype(f32)).astype(bf16)
    if tail:
        total = keep_ref[2 * half :] + recv_ref[2 * half :].astype(f32)
        kept_ref[half:] = total
        send_ref[half:] = total.astype(bf16)


def halve(keep, recv, tail):
    half = (keep.shape[0] - tail) // 2 + tail
    shape = (half, keep.shape[1])
    return in_vmem(functools.partial(halve_body, tail), "halve", [(shape, f32), (shape, bf16)], keep, recv)


def hidden_body(keep_ref, recv_ref, gate_factor_ref, up_factor_ref, down_factor_ref, out_ref):
    size = gate_factor_ref.shape[0]
    total = keep_ref[...] + recv_ref[...].astype(f32)
    rank = total[2 * size :].astype(bf16)
    sums = []
    for i, factor_ref in enumerate((gate_factor_ref, up_factor_ref)):
        term = jnp.dot(factor_ref[...], rank[RANK * i : RANK * i + RANK], preferred_element_type=f32)
        sums.append(total[i * size : (i + 1) * size] + adapter_scale * term)
    gate, up = sums
    hidden = (gate / (1.0 + jnp.exp(-gate)) * up).astype(bf16)
    low = jnp.dot(down_factor_ref[...], hidden, preferred_element_type=f32).astype(bf16)
    for copy in range(out_ref.shape[0]):
        out_ref[copy, :size] = hidden
        out_ref[copy, size:] = low


def join_body(tail, mine_ref, theirs_ref, out_ref):
    size = mine_ref.shape[0] - tail
    out_ref[:size] = mine_ref[:size]
    out_ref[size : 2 * size] = theirs_ref[:size]
    out_ref[2 * size :] = (mine_ref[size:].astype(f32) + theirs_ref[size:].astype(f32)).astype(bf16)


def join(mine, theirs):
    size = mine.shape[0] - RANK
    shape = (2 * size + RANK, mine.shape[1])
    return in_vmem(functools.partial(join_body, RANK), "join", [(shape, bf16)], mine, theirs)[0]


def spread_body(mine_ref, theirs_ref, out_ref, rank_ref):
    size = (mine_ref.shape[0] - RANK) // 8
    for r in range(16):
        from_ref = theirs_ref if r >> 3 else mine_ref
        at = (r & 7) * size
        out_ref[rows_at(fsdp_owner(r, False), size), :] = from_ref[at : at + size]
    rank_ref[...] = (mine_ref[8 * size :].astype(f32) + theirs_ref[8 * size :].astype(f32)).astype(bf16)


def chip_spread_body(mine_ref, theirs_ref, out_ref, rank_ref):
    chips, size = mine_ref.shape[0], mine_ref.shape[1] - RANK
    core = lax.axis_index("c")
    low = jnp.zeros(rank_ref.shape, f32)
    for chip in range(chips):
        for side, from_ref in enumerate((mine_ref, theirs_ref)):
            out_ref[rows_at(2 * chip + (core if side == 0 else 1 - core), size), :] = from_ref[chip, :size]
            low = low + from_ref[chip, size:].astype(f32)
    rank_ref[...] = low.astype(bf16)


def tp_order_body(part_ref, rank_ref, factor_ref, keep_ref, send_ref, total_ref):
    size = part_ref.shape[0] // 8
    total_ref[...] = part_ref[...] + adapter_scale * lax.dot_general(
        rank_ref[...], factor_ref[...], (((0,), (0,)), ((), ())), preferred_element_type=f32
    )
    for q in range(8):
        block = total_ref[rows_at(tp_owner(q), size), :]
        if q < 4:
            keep_ref[q * size : (q + 1) * size] = block
        else:
            send_ref[(q - 4) * size : (q - 3) * size] = block.astype(bf16)


def last_body(keep_ref, recv_ref, out_ref):
    out_ref[...] = (keep_ref[...] + recv_ref[...].astype(f32)).astype(bf16)


def last_both_body(keep_ref, recv_ref, earlier_ref, out_ref):
    out_ref[0] = earlier_ref[...]
    out_ref[1] = (keep_ref[...] + recv_ref[...].astype(f32)).astype(bf16)


def after(value, earlier):
    return lax.optimization_barrier((value, earlier))[0]


def per_device(
    normed,
    resident_gate_matrix,
    resident_up_matrix,
    resident_down_matrix,
    gate_input_factor,
    up_input_factor,
    gate_output_factor,
    up_output_factor,
    down_input_factor,
    down_output_factor,
):
    steps, rows, depth = normed.shape
    units = resident_gate_matrix.shape[1]
    size = units // 16

    states = normed.reshape(steps * rows, depth)

    def times(matrix, value):
        return lax.dot_general(matrix, value, (((0,), (1,)), ((), ())), preferred_element_type=f32).astype(bf16)

    wide = jnp.concatenate([gate_input_factor, up_input_factor, down_output_factor.T], 0)
    wide = exchange(TP, jnp.broadcast_to(wide, (8, *wide.shape)))
    wide = wide.transpose(1, 0, 2).reshape(wide.shape[1], -1)
    up = times(resident_up_matrix, states)
    gate = times(resident_gate_matrix, states)
    recvs = []
    for s in range(steps):
        (send,) = in_vmem(
            functools.partial(other_core_body, size, s), "other_core", [((units, rows), bf16)], gate, up
        )
        recvs.append(swap("c", send))
    rank = lax.dot_general(
        wide[: 2 * RANK], states, (((1,), (1,)), ((), ())), preferred_element_type=f32
    )
    rank_recv = swap("c", rank)
    near, far, across = (
        functools.partial(ring_pair, "z", True),
        functools.partial(ring_pair, "z", False),
        functools.partial(swap, "yh"),
    )

    def step_chain(s):
        shape = (8 * size + 2 * RANK, rows)
        keep, send = in_vmem(
            functools.partial(core_sum_body, size, s),
            "core_sum",
            [(shape, f32), (shape, bf16)],
            gate,
            up,
            recvs[s],
            rank,
            rank_recv,
        )
        route = (across, near, far) if s else (near, far, across)
        keep, send = halve(keep, (yield route[0], send), 2 * RANK)
        keep, send = halve(keep, (yield route[1], send), 2 * RANK)
        (hidden,) = in_vmem(
            hidden_body,
            "hidden",
            [((8 if s else 1, size + RANK, rows), bf16)],
            keep,
            (yield route[2], send),
            gate_output_factor,
            up_output_factor,
            down_input_factor,
        )
        if s:
            hidden = yield functools.partial(exchange, ("yh", "z")), hidden
        else:
            hidden = hidden[0]
            for move in (across, far, near):
                hidden = join(hidden, (yield move, hidden))
        hidden, rank_down = in_vmem(
            chip_spread_body if s else spread_body,
            "spread",
            [((units, rows), bf16), ((RANK, rows), bf16)],
            hidden,
            (yield functools.partial(swap, "c"), hidden),
        )
        part = lax.dot_general(
            hidden, resident_down_matrix, (((0,), (0,)), ((), ())), preferred_element_type=f32
        )
        half = (rows // 2, part.shape[1])
        keep, send = in_vmem(
            tp_order_body,
            "tp_order",
            [(half, f32), (half, bf16)],
            part,
            rank_down,
            wide[2 * RANK :],
            scratch=[pltpu.VMEM(part.shape, f32)],
        )
        keep, send = halve(keep, (yield functools.partial(ring_pair, "x", True), send), 0)
        keep, send = halve(keep, (yield functools.partial(ring_pair, "x", False), send), 0)
        return keep, (yield functools.partial(swap, "yl"), send)

    chains = [step_chain(s) for s in range(steps)]
    waiting = [next(chain) for chain in chains]
    sums = [None] * steps
    earlier = None
    for turn in ORDER:
        move, value = waiting[turn]
        if earlier is not None:
            value = after(value, earlier)
        earlier = value
        try:
            waiting[turn] = chains[turn].send(move(value))
        except StopIteration as end:
            sums[turn] = end.value
    (first,) = in_vmem(last_body, "last", [(sums[0][0].shape, bf16)], *sums[0])
    (both,) = in_vmem(last_both_body, "last_both", [((2, *first.shape), bf16)], *sums[1], first)
    return both


def solution(mesh):
    fine = Mesh(mesh.devices.reshape(2, 4, 2, 4, 2), FSDP + TP)
    fsdp, tp = FSDP, TP
    in_specs = (
        P(None, None, fsdp),
        P(fsdp, tp),
        P(fsdp, tp),
        P(tp, fsdp),
        P(None, fsdp + tp),
        P(None, fsdp + tp),
        P(tp + fsdp, None),
        P(tp + fsdp, None),
        P(None, tp + fsdp),
        P(fsdp + tp, None),
    )
    out_specs = P(None, tp, fsdp)
    return jax.shard_map(
        per_device, mesh=fine, in_specs=in_specs, out_specs=out_specs, check_vma=False
    )
```

```python
import functools

import jax
import jax.numpy as jnp
from jax import lax
from jax.experimental import pallas as pl
from jax.experimental.pallas import tpu as pltpu
from jax.sharding import Mesh
from jax.sharding import PartitionSpec as P

adapter_scale = 2.0
f32 = jnp.float32
bf16 = jnp.bfloat16
FSDP = ("yh", "z", "c")
TP = ("x", "yl")
RANK = 16
VMEM_LIMIT = 16 * 1024 * 1024


def pair_bits(core):
    return 1 + 2 * core, 3 - 2 * core


def owner(r, y_first):
    yh, z, c = lax.axis_index("yh"), lax.axis_index("z"), lax.axis_index("c")
    core, bits = (r >> 3) & 1, ((r >> 2) & 1, (r >> 1) & 1, r & 1)
    y, first_z, second_z = bits if y_first else (bits[2], bits[0], bits[1])
    cc = c ^ core
    a, b = pair_bits(cc)
    zz = z ^ (first_z * a) ^ (second_z * b)
    return ((yh ^ y) * 4 + zz) * 2 + cc


def swap(axis, value):
    return lax.ppermute(value, axis, [(0, 1), (1, 0)])


def ring_pair(axis, first, value):
    axes = ("z", "c") if axis == "z" else ("c", "x")

    def index(place, core):
        return place * 2 + core if axis == "z" else core * 4 + place

    moves = []
    for place in range(4):
        for core in range(2):
            step = pair_bits(core)[0 if first else 1]
            moves.append((index(place, core), index(place ^ step, core)))
    return lax.ppermute(value, axes, moves)


def xor_pair(axis, step, value):
    return lax.ppermute(value, axis, [(i, i ^ step) for i in range(4)])


def exchange(axes, value):
    return lax.all_to_all(value, axes, split_axis=0, concat_axis=0)


def in_vmem(body, name, out_shape, *args, behind=(), token=False):
    whole = pl.BlockSpec(memory_space=pltpu.VMEM)
    if token:
        out_shape = (*out_shape, ((8, 128), f32))
    outs = tuple(jax.ShapeDtypeStruct(shape, dtype) for shape, dtype in out_shape)
    moved = sum(a.size * a.dtype.itemsize for a in (*args, *outs))

    def kernel(*refs):
        out_refs = refs[len(args) + len(behind) :]
        if token:
            out_refs[-1][...] = jnp.zeros((8, 128), f32)
            out_refs = out_refs[:-1]
        body(*refs[: len(args)], *out_refs)

    return pl.pallas_call(
        kernel,
        in_specs=[whole] * (len(args) + len(behind)),
        out_specs=[whole] * len(outs),
        out_shape=outs,
        compiler_params=pltpu.CompilerParams(vmem_limit_bytes=VMEM_LIMIT),
        cost_estimate=pl.CostEstimate(flops=moved, bytes_accessed=moved, transcendentals=0),
        name=name,
    )(*args, *behind)


def rows_at(block, size):
    return pl.ds(pl.multiple_of(block * size, 16), size)


def other_core_body(size, y_first, part_ref, send_ref):
    for r in range(8):
        send_ref[r * size : (r + 1) * size] = part_ref[rows_at(owner(8 + r, y_first), size), :]


def core_sum_body(size, y_first, part_ref, recv_ref, keep_ref, send_ref):
    for r in range(8):
        at = r * size
        mine = rows_at(owner(r, y_first), size)
        total = part_ref[mine, :].astype(f32) + recv_ref[at : at + size].astype(f32)
        if r < 4:
            keep_ref[at : at + size] = total
        else:
            send_ref[at - 4 * size : at - 3 * size] = total.astype(bf16)


def halve_body(keep_ref, recv_ref, kept_ref, send_ref):
    half = kept_ref.shape[0]
    kept_ref[...] = keep_ref[:half] + recv_ref[:half].astype(f32)
    send_ref[...] = (keep_ref[half:] + recv_ref[half:].astype(f32)).astype(bf16)


def halve_joined_body(keep_ref, recv_ref, rank_ref, rank_recv_ref, kept_ref, send_ref):
    half = keep_ref.shape[0] // 2
    kept_ref[:half] = keep_ref[:half] + recv_ref[:half].astype(f32)
    send_ref[:half] = (keep_ref[half:] + recv_ref[half:].astype(f32)).astype(bf16)
    rank = rank_ref[...] + rank_recv_ref[...]
    kept_ref[half:] = rank
    send_ref[half:] = rank.astype(bf16)


def halve_tail_body(keep_ref, recv_ref, kept_ref, send_ref):
    half = kept_ref.shape[0] - 2 * RANK
    kept_ref[:half] = keep_ref[:half] + recv_ref[:half].astype(f32)
    send_ref[:half] = (keep_ref[half : 2 * half] + recv_ref[half : 2 * half].astype(f32)).astype(bf16)
    total = keep_ref[2 * half :] + recv_ref[2 * half :].astype(f32)
    kept_ref[half:] = total
    send_ref[half:] = total.astype(bf16)


def halve(body, half, *args):
    shape = (half, args[0].shape[1])
    return in_vmem(body, "halve", [(shape, f32), (shape, bf16)], *args)


def hidden_body(
    gate_ref, gate_recv_ref, up_ref, up_recv_ref, gate_factor_ref, up_factor_ref, down_factor_ref, out_ref
):
    size = gate_factor_ref.shape[1]
    rank = (up_ref[size:] + up_recv_ref[size:].astype(f32)).astype(bf16)
    gate = lax.dot_general(
        gate_factor_ref[...], rank[:RANK], (((0,), (0,)), ((), ())), preferred_element_type=f32
    )
    gate = gate_ref[...] + gate_recv_ref[...].astype(f32) + adapter_scale * gate
    up = lax.dot_general(up_factor_ref[...], rank[RANK:], (((0,), (0,)), ((), ())), preferred_element_type=f32)
    up = up_ref[:size] + up_recv_ref[:size].astype(f32) + adapter_scale * up
    hidden = (gate / (1.0 + jnp.exp(-gate)) * up).astype(bf16)
    low = jnp.dot(down_factor_ref[...], hidden, preferred_element_type=f32).astype(bf16)
    for copy in range(out_ref.shape[0]):
        out_ref[copy, :size] = hidden
        out_ref[copy, size:] = low


def double_body(bit, mine_ref, theirs_ref, out_ref):
    count = mine_ref.shape[0]
    high = bit()
    out_ref[pl.ds(high * count, count)] = mine_ref[...]
    out_ref[pl.ds((1 - high) * count, count)] = theirs_ref[...]


def double_flat_body(bit, mine_ref, theirs_ref, out_ref):
    count, _, width = mine_ref.shape
    high = bit()
    for side, from_ref in ((high, mine_ref), (1 - high, theirs_ref)):
        for i in range(count):
            at = pl.multiple_of((side * count + i) * width, width)
            out_ref[:, pl.ds(at, width)] = from_ref[i]


def add_body(mine_ref, theirs_ref, out_ref):
    out_ref[...] = mine_ref[...] + theirs_ref[...]


def spread_body(mine_ref, theirs_ref, out_ref, low_ref):
    chips, size = mine_ref.shape[0], mine_ref.shape[1] - RANK
    core = lax.axis_index("c")
    low = jnp.zeros(low_ref.shape, f32)
    for chip in range(chips):
        for side, from_ref in enumerate((mine_ref, theirs_ref)):
            out_ref[rows_at(2 * chip + (core if side == 0 else 1 - core), size), :] = from_ref[chip, :size]
            low = low + from_ref[chip, size:].astype(f32)
    low_ref[...] = low.astype(bf16)


def tp_blocks_body(part_ref, low_ref, factor_ref, out_ref):
    blocks, steps, block = out_ref.shape[:3]
    for s in range(steps):
        first = s * blocks * block
        rows = slice(first, first + blocks * block)
        term = lax.dot_general(
            low_ref[:, rows], factor_ref[2 * RANK :], (((0,), (0,)), ((), ())), preferred_element_type=f32
        )
        total = (part_ref[rows] + adapter_scale * term).astype(bf16)
        for t in range(blocks):
            out_ref[t, s] = total[t * block : (t + 1) * block]


def owner_sum_body(blocks_ref, out_ref):
    total = blocks_ref[0].astype(f32)
    for t in range(1, blocks_ref.shape[0]):
        total = total + blocks_ref[t].astype(f32)
    out_ref[...] = total.astype(bf16)


def after(value, earlier):
    return lax.optimization_barrier((value, earlier))[0]


def per_device(
    normed,
    resident_gate_matrix,
    resident_up_matrix,
    resident_down_matrix,
    gate_input_factor,
    up_input_factor,
    gate_output_factor,
    up_output_factor,
    down_input_factor,
    down_output_factor,
):
    steps, rows, depth = normed.shape
    units = resident_gate_matrix.shape[1]
    size = units // 16
    lanes = steps * rows
    states = normed.reshape(lanes, depth)
    near, far, across = (
        functools.partial(ring_pair, "z", True),
        functools.partial(ring_pair, "z", False),
        functools.partial(swap, "yh"),
    )

    wide = jnp.concatenate([gate_input_factor, up_input_factor, down_output_factor.T], 0)[None]
    (wide,) = in_vmem(
        functools.partial(double_body, lambda: lax.axis_index("yl")),
        "double",
        [((2, *wide.shape[1:]), bf16)],
        wide,
        swap("yl", wide),
    )
    parts = [
        lax.dot_general(w, states, (((0,), (1,)), ((), ())), preferred_element_type=f32).astype(bf16)
        for w in (resident_gate_matrix, resident_up_matrix)
    ]
    recvs, sums, tokens = [], [], []
    for part, y_first in zip(parts, (True, False)):
        (send,) = in_vmem(
            functools.partial(other_core_body, size, y_first), "other_core", [((units // 2, lanes), bf16)], part, behind=(wide,)
        )
        recvs.append(swap("c", send))
    for part, recv, y_first in zip(parts, recvs, (True, False)):
        shape = (4 * size, lanes)
        keep, send, token = in_vmem(
            functools.partial(core_sum_body, size, y_first),
            "core_sum",
            [(shape, f32), (shape, bf16)],
            part,
            recv,
            behind=tokens,
            token=True,
        )
        sums.append((keep, send))
        tokens = [token]
    wide = after(wide, token)
    (wide,) = in_vmem(
        functools.partial(double_body, lambda: lax.axis_index("x") & 1),
        "double",
        [((4, *wide.shape[1:]), bf16)],
        wide,
        xor_pair("x", 1, wide),
    )
    (wide,) = in_vmem(
        functools.partial(double_flat_body, lambda: lax.axis_index("x") >> 1),
        "double",
        [((3 * RANK, depth), bf16)],
        wide,
        xor_pair("x", 3, wide),
    )
    rank = lax.dot_general(
        wide[: 2 * RANK], states, (((1,), (1,)), ((), ())), preferred_element_type=f32
    )
    (rank,) = in_vmem(add_body, "add", [(rank.shape, f32)], rank, swap("c", rank))

    keep, send = sums[0]
    keep, send = halve(halve_body, 2 * size, keep, across(send))
    keep, send = halve(halve_body, size, keep, near(send))
    gate = keep, far(send)
    keep, send = sums[1]
    keep, send = halve(halve_joined_body, 2 * size + 2 * RANK, keep, near(send), rank, near(rank))
    keep, send = halve(halve_tail_body, size + 2 * RANK, keep, far(send))
    up = keep, across(send)
    (hidden,) = in_vmem(
        hidden_body,
        "hidden",
        [((8, size + RANK, lanes), bf16)],
        *gate,
        *up,
        gate_output_factor.T,
        up_output_factor.T,
        down_input_factor,
    )
    hidden = exchange(("yh", "z"), hidden)
    hidden, low = in_vmem(
        spread_body, "spread", [((units, lanes), bf16), ((RANK, lanes), bf16)], hidden, swap("c", hidden)
    )
    part = lax.dot_general(
        hidden, resident_down_matrix, (((0,), (0,)), ((), ())), preferred_element_type=f32
    )
    (blocks,) = in_vmem(
        tp_blocks_body,
        "tp_blocks",
        [((8, steps, rows // 8, part.shape[1]), bf16)],
        part,
        low,
        wide,
    )
    blocks = exchange(TP, blocks)
    return in_vmem(owner_sum_body, "owner_sum", [(blocks.shape[1:], bf16)], blocks)[0]


def solution(mesh):
    fine = Mesh(mesh.devices.reshape(2, 4, 2, 4, 2), FSDP + TP)
    fsdp, tp = FSDP, TP
    in_specs = (
        P(None, None, fsdp),
        P(fsdp, tp),
        P(fsdp, tp),
        P(tp, fsdp),
        P(None, fsdp + tp),
        P(None, fsdp + tp),
        P(tp + fsdp, None),
        P(tp + fsdp, None),
        P(None, tp + fsdp),
        P(fsdp + tp, None),
    )
    out_specs = P(None, tp, fsdp)
    return jax.shard_map(
        per_device, mesh=fine, in_specs=in_specs, out_specs=out_specs, check_vma=False
    )
```

```python
import functools

import jax
import jax.numpy as jnp
from jax import lax
from jax.experimental import pallas as pl
from jax.experimental.pallas import tpu as pltpu
from jax.sharding import Mesh
from jax.sharding import PartitionSpec as P

adapter_scale = 2.0
f32 = jnp.float32
bf16 = jnp.bfloat16
FSDP = ("yh", "z", "c")
TP = ("x", "yl")
RANK = 16
VMEM_LIMIT = 16 * 1024 * 1024


def pair_bits(core):
    return 1 + 2 * core, 3 - 2 * core


def owner(r, y_first):
    yh, z, c = lax.axis_index("yh"), lax.axis_index("z"), lax.axis_index("c")
    core, bits = (r >> 3) & 1, ((r >> 2) & 1, (r >> 1) & 1, r & 1)
    y, first_z, second_z = bits if y_first else (bits[2], bits[0], bits[1])
    cc = c ^ core
    a, b = pair_bits(cc)
    zz = z ^ (first_z * a) ^ (second_z * b)
    return ((yh ^ y) * 4 + zz) * 2 + cc


def swap(axis, value):
    return lax.ppermute(value, axis, [(0, 1), (1, 0)])


def ring_pair(axis, first, value):
    axes = ("z", "c") if axis == "z" else ("c", "x")

    def index(place, core):
        return place * 2 + core if axis == "z" else core * 4 + place

    moves = []
    for place in range(4):
        for core in range(2):
            step = pair_bits(core)[0 if first else 1]
            moves.append((index(place, core), index(place ^ step, core)))
    return lax.ppermute(value, axes, moves)


def xor_pair(axis, step, value):
    return lax.ppermute(value, axis, [(i, i ^ step) for i in range(4)])


def exchange(axes, value):
    return lax.all_to_all(value, axes, split_axis=0, concat_axis=0)


def in_vmem(body, name, out_shape, *args, behind=(), token=False):
    whole = pl.BlockSpec(memory_space=pltpu.VMEM)
    if token:
        out_shape = (*out_shape, ((8, 128), f32))
    outs = tuple(jax.ShapeDtypeStruct(shape, dtype) for shape, dtype in out_shape)
    moved = sum(a.size * a.dtype.itemsize for a in (*args, *outs))

    def kernel(*refs):
        out_refs = refs[len(args) + len(behind) :]
        if token:
            out_refs[-1][...] = jnp.zeros((8, 128), f32)
            out_refs = out_refs[:-1]
        body(*refs[: len(args)], *out_refs)

    return pl.pallas_call(
        kernel,
        in_specs=[whole] * (len(args) + len(behind)),
        out_specs=[whole] * len(outs),
        out_shape=outs,
        compiler_params=pltpu.CompilerParams(vmem_limit_bytes=VMEM_LIMIT),
        cost_estimate=pl.CostEstimate(flops=moved, bytes_accessed=moved, transcendentals=0),
        name=name,
    )(*args, *behind)


def rows_at(block, size):
    return pl.ds(pl.multiple_of(block * size, 16), size)


def other_core_body(size, y_first, part_ref, send_ref):
    for r in range(8):
        send_ref[r * size : (r + 1) * size] = part_ref[rows_at(owner(8 + r, y_first), size), :]


def core_sum_body(size, y_first, part_ref, recv_ref, keep_ref, send_ref):
    for r in range(8):
        at = r * size
        mine = rows_at(owner(r, y_first), size)
        total = part_ref[mine, :].astype(f32) + recv_ref[at : at + size].astype(f32)
        if r < 4:
            keep_ref[at : at + size] = total
        else:
            send_ref[at - 4 * size : at - 3 * size] = total.astype(bf16)


def halve_body(keep_ref, recv_ref, kept_ref, send_ref):
    half = kept_ref.shape[0]
    kept_ref[...] = keep_ref[:half] + recv_ref[:half].astype(f32)
    send_ref[...] = (keep_ref[half:] + recv_ref[half:].astype(f32)).astype(bf16)


def halve_joined_body(keep_ref, recv_ref, rank_ref, rank_recv_ref, kept_ref, send_ref):
    half = keep_ref.shape[0] // 2
    kept_ref[:half] = keep_ref[:half] + recv_ref[:half].astype(f32)
    send_ref[:half] = (keep_ref[half:] + recv_ref[half:].astype(f32)).astype(bf16)
    rank = rank_ref[...] + rank_recv_ref[...]
    kept_ref[half:] = rank
    send_ref[half:] = rank.astype(bf16)


def halve_tail_body(keep_ref, recv_ref, kept_ref, send_ref):
    half = kept_ref.shape[0] - 2 * RANK
    kept_ref[:half] = keep_ref[:half] + recv_ref[:half].astype(f32)
    send_ref[:half] = (keep_ref[half : 2 * half] + recv_ref[half : 2 * half].astype(f32)).astype(bf16)
    total = keep_ref[2 * half :] + recv_ref[2 * half :].astype(f32)
    kept_ref[half:] = total
    send_ref[half:] = total.astype(bf16)


def halve(body, half, *args, behind=()):
    shape = (half, args[0].shape[1])
    return in_vmem(body, "halve", [(shape, f32), (shape, bf16)], *args, behind=behind)


def hidden_body(
    gate_ref, gate_recv_ref, up_ref, up_recv_ref, gate_factor_ref, up_factor_ref, down_factor_ref, out_ref
):
    size = gate_factor_ref.shape[1]
    rank = (up_ref[size:] + up_recv_ref[size:].astype(f32)).astype(bf16)
    gate = lax.dot_general(
        gate_factor_ref[...], rank[:RANK], (((0,), (0,)), ((), ())), preferred_element_type=f32
    )
    gate = gate_ref[...] + gate_recv_ref[...].astype(f32) + adapter_scale * gate
    up = lax.dot_general(up_factor_ref[...], rank[RANK:], (((0,), (0,)), ((), ())), preferred_element_type=f32)
    up = up_ref[:size] + up_recv_ref[:size].astype(f32) + adapter_scale * up
    hidden = (gate / (1.0 + jnp.exp(-gate)) * up).astype(bf16)
    low = jnp.dot(down_factor_ref[...], hidden, preferred_element_type=f32).astype(bf16)
    for copy in range(out_ref.shape[0]):
        out_ref[copy, :size] = hidden
        out_ref[copy, size:] = low


def double_body(bit, mine_ref, theirs_ref, out_ref):
    count = mine_ref.shape[0]
    high = bit()
    out_ref[pl.ds(high * count, count)] = mine_ref[...]
    out_ref[pl.ds((1 - high) * count, count)] = theirs_ref[...]


def double_flat_body(bit, mine_ref, theirs_ref, out_ref):
    count, _, width = mine_ref.shape
    high = bit()
    for side, from_ref in ((high, mine_ref), (1 - high, theirs_ref)):
        for i in range(count):
            at = pl.multiple_of((side * count + i) * width, width)
            out_ref[:, pl.ds(at, width)] = from_ref[i]


def add_body(mine_ref, theirs_ref, out_ref):
    out_ref[...] = mine_ref[...] + theirs_ref[...]


def strip_body(from_ref, out_ref, low_ref):
    chips, size = from_ref.shape[0], from_ref.shape[1] - RANK
    low = jnp.zeros(low_ref.shape, f32)
    for chip in range(chips):
        out_ref[chip * size : (chip + 1) * size] = from_ref[chip, :size]
        low = low + from_ref[chip, size:].astype(f32)
    low_ref[...] = low


def down_rows_body(size, down_ref, own_ref, other_ref, token_ref, sem):
    core = lax.axis_index("c")
    token_ref[...] = jnp.zeros(token_ref.shape, f32)
    copies = []
    for side, to_ref in enumerate((own_ref, other_ref)):
        for chip in range(8):
            copies.append(
                pltpu.make_async_copy(
                    down_ref.at[rows_at(2 * chip + (core if side == 0 else 1 - core), size)],
                    to_ref.at[pl.ds(chip * size, size)],
                    sem.at[side * 8 + chip],
                )
            )
    for copy in copies:
        copy.start()
    for copy in copies:
        copy.wait()


def down_rows(size, down):
    units, width = down.shape
    half = jax.ShapeDtypeStruct((units // 2, width), down.dtype)
    whole = pl.BlockSpec(memory_space=pltpu.VMEM)
    return pl.pallas_call(
        functools.partial(down_rows_body, size),
        in_specs=[pl.BlockSpec(memory_space=pl.ANY)],
        out_specs=[whole] * 3,
        out_shape=[half, half, jax.ShapeDtypeStruct((8, 128), f32)],
        scratch_shapes=[pltpu.SemaphoreType.DMA((16,))],
        compiler_params=pltpu.CompilerParams(vmem_limit_bytes=VMEM_LIMIT),
        cost_estimate=pl.CostEstimate(flops=0, bytes_accessed=4 * units * width, transcendentals=0),
        name="down_rows",
    )(down)


def tp_blocks_body(own_ref, own_low_ref, other_ref, other_low_ref, factor_ref, out_ref):
    blocks, steps, block = out_ref.shape[:3]
    low = (own_low_ref[...] + other_low_ref[...]).astype(bf16)
    for s in range(steps):
        first = s * blocks * block
        rows = slice(first, first + blocks * block)
        term = lax.dot_general(
            low[:, rows], factor_ref[2 * RANK :], (((0,), (0,)), ((), ())), preferred_element_type=f32
        )
        total = (own_ref[rows] + other_ref[rows] + adapter_scale * term).astype(bf16)
        for t in range(blocks):
            out_ref[t, s] = total[t * block : (t + 1) * block]


def owner_sum_body(blocks_ref, out_ref):
    total = blocks_ref[0].astype(f32)
    for t in range(1, blocks_ref.shape[0]):
        total = total + blocks_ref[t].astype(f32)
    out_ref[...] = total.astype(bf16)


def per_device(
    normed,
    resident_gate_matrix,
    resident_up_matrix,
    resident_down_matrix,
    gate_input_factor,
    up_input_factor,
    gate_output_factor,
    up_output_factor,
    down_input_factor,
    down_output_factor,
):
    steps, rows, depth = normed.shape
    units = resident_gate_matrix.shape[1]
    size = units // 16
    lanes = steps * rows
    states = normed.reshape(lanes, depth)
    near, far, across = (
        functools.partial(ring_pair, "z", True),
        functools.partial(ring_pair, "z", False),
        functools.partial(swap, "yh"),
    )

    wide = jnp.concatenate([gate_input_factor, up_input_factor, down_output_factor.T], 0)[None]
    (wide,) = in_vmem(
        functools.partial(double_body, lambda: lax.axis_index("yl")),
        "double",
        [((2, *wide.shape[1:]), bf16)],
        wide,
        swap("yl", wide),
    )
    parts = [
        lax.dot_general(w, states, (((0,), (1,)), ((), ())), preferred_element_type=f32).astype(bf16)
        for w in (resident_gate_matrix, resident_up_matrix)
    ]
    recvs, sums, tokens = [], [], []
    for part, y_first in zip(parts, (True, False)):
        (send,) = in_vmem(
            functools.partial(other_core_body, size, y_first), "other_core", [((units // 2, lanes), bf16)], part
        )
        recvs.append(swap("c", send))
    for part, recv, y_first in zip(parts, recvs, (True, False)):
        shape = (4 * size, lanes)
        keep, send, token = in_vmem(
            functools.partial(core_sum_body, size, y_first),
            "core_sum",
            [(shape, f32), (shape, bf16)],
            part,
            recv,
            behind=tokens,
            token=True,
        )
        sums.append((keep, send))
        tokens = [token, wide]
    (wide,) = in_vmem(
        functools.partial(double_body, lambda: lax.axis_index("x") & 1),
        "double",
        [((4, *wide.shape[1:]), bf16)],
        wide,
        xor_pair("x", 1, wide),
    )
    (wide,) = in_vmem(
        functools.partial(double_flat_body, lambda: lax.axis_index("x") >> 1),
        "double",
        [((3 * RANK, depth), bf16)],
        wide,
        xor_pair("x", 3, wide),
    )
    rank = lax.dot_general(
        wide[: 2 * RANK], states, (((1,), (1,)), ((), ())), preferred_element_type=f32
    )
    (rank,) = in_vmem(add_body, "add", [(rank.shape, f32)], rank, swap("c", rank))

    *down, token = down_rows(size, resident_down_matrix)
    keep, send = sums[0]
    keep, send = halve(halve_body, 2 * size, keep, across(send))
    keep, send = halve(halve_body, size, keep, near(send))
    gate = keep, far(send)
    keep, send = sums[1]
    keep, send = halve(halve_joined_body, 2 * size + 2 * RANK, keep, near(send), rank, near(rank))
    keep, send = halve(halve_tail_body, size + 2 * RANK, keep, far(send), behind=(token,))
    up = keep, across(send)
    (hidden,) = in_vmem(
        hidden_body,
        "hidden",
        [((8, size + RANK, lanes), bf16)],
        *gate,
        *up,
        gate_output_factor.T,
        up_output_factor.T,
        down_input_factor,
    )
    hidden = exchange(("yh", "z"), hidden)
    pieces = []
    for value, matrix in zip((hidden, swap("c", hidden)), down):
        value, low = in_vmem(
            strip_body, "strip", [((units // 2, lanes), bf16), ((RANK, lanes), f32)], value
        )
        part = lax.dot_general(value, matrix, (((0,), (0,)), ((), ())), preferred_element_type=f32)
        pieces += [part, low]
    (blocks,) = in_vmem(
        tp_blocks_body, "tp_blocks", [((8, steps, rows // 8, depth), bf16)], *pieces, wide
    )
    blocks = exchange(TP, blocks)
    return in_vmem(owner_sum_body, "owner_sum", [(blocks.shape[1:], bf16)], blocks)[0]


def solution(mesh):
    fine = Mesh(mesh.devices.reshape(2, 4, 2, 4, 2), FSDP + TP)
    fsdp, tp = FSDP, TP
    in_specs = (
        P(None, None, fsdp),
        P(fsdp, tp),
        P(fsdp, tp),
        P(tp, fsdp),
        P(None, fsdp + tp),
        P(None, fsdp + tp),
        P(tp + fsdp, None),
        P(tp + fsdp, None),
        P(None, tp + fsdp),
        P(fsdp + tp, None),
    )
    out_specs = P(None, tp, fsdp)
    return jax.shard_map(
        per_device, mesh=fine, in_specs=in_specs, out_specs=out_specs, check_vma=False
    )
```

```python
import functools

import jax
import jax.numpy as jnp
from jax import lax
from jax.experimental import pallas as pl
from jax.experimental.pallas import tpu as pltpu
from jax.sharding import Mesh
from jax.sharding import PartitionSpec as P

adapter_scale = 2.0
f32 = jnp.float32
bf16 = jnp.bfloat16
FSDP = ("yh", "z", "c")
TP = ("x", "yl")
RANK = 16
VMEM_LIMIT = 16 * 1024 * 1024


def pair_bits(core):
    return 1 + 2 * core, 3 - 2 * core


def owner(r, y_first):
    yh, z, c = lax.axis_index("yh"), lax.axis_index("z"), lax.axis_index("c")
    core, bits = (r >> 3) & 1, ((r >> 2) & 1, (r >> 1) & 1, r & 1)
    y, first_z, second_z = bits if y_first else (bits[2], bits[0], bits[1])
    cc = c ^ core
    a, b = pair_bits(cc)
    zz = z ^ (first_z * a) ^ (second_z * b)
    return ((yh ^ y) * 4 + zz) * 2 + cc


def swap(axis, value):
    return lax.ppermute(value, axis, [(0, 1), (1, 0)])


def ring_pair(axis, first, value):
    axes = ("z", "c") if axis == "z" else ("c", "x")

    def index(place, core):
        return place * 2 + core if axis == "z" else core * 4 + place

    moves = []
    for place in range(4):
        for core in range(2):
            step = pair_bits(core)[0 if first else 1]
            moves.append((index(place, core), index(place ^ step, core)))
    return lax.ppermute(value, axes, moves)


def xor_pair(axis, step, value):
    return lax.ppermute(value, axis, [(i, i ^ step) for i in range(4)])


def exchange(axes, value):
    return lax.all_to_all(value, axes, split_axis=0, concat_axis=0)


def in_vmem(body, name, out_shape, *args, behind=(), token=False):
    whole = pl.BlockSpec(memory_space=pltpu.VMEM)
    if token:
        out_shape = (*out_shape, ((8, 128), f32))
    outs = tuple(jax.ShapeDtypeStruct(shape, dtype) for shape, dtype in out_shape)
    moved = sum(a.size * a.dtype.itemsize for a in (*args, *outs))

    def kernel(*refs):
        out_refs = refs[len(args) + len(behind) :]
        if token:
            out_refs[-1][...] = jnp.zeros((8, 128), f32)
            out_refs = out_refs[:-1]
        body(*refs[: len(args)], *out_refs)

    return pl.pallas_call(
        kernel,
        in_specs=[whole] * (len(args) + len(behind)),
        out_specs=[whole] * len(outs),
        out_shape=outs,
        compiler_params=pltpu.CompilerParams(vmem_limit_bytes=VMEM_LIMIT),
        cost_estimate=pl.CostEstimate(flops=moved, bytes_accessed=moved, transcendentals=0),
        name=name,
    )(*args, *behind)


def rows_at(block, size):
    return pl.ds(pl.multiple_of(block * size, 16), size)


def other_core_body(size, y_first, part_ref, send_ref):
    for r in range(8):
        send_ref[r * size : (r + 1) * size] = part_ref[rows_at(owner(8 + r, y_first), size), :]


def core_sum_body(size, y_first, part_ref, recv_ref, keep_ref, send_ref):
    for r in range(8):
        at = r * size
        mine = rows_at(owner(r, y_first), size)
        total = part_ref[mine, :].astype(f32) + recv_ref[at : at + size].astype(f32)
        if r < 4:
            keep_ref[at : at + size] = total
        else:
            send_ref[at - 4 * size : at - 3 * size] = total.astype(bf16)


def halve_body(keep_ref, recv_ref, kept_ref, send_ref):
    half = kept_ref.shape[0]
    kept_ref[...] = keep_ref[:half] + recv_ref[:half].astype(f32)
    send_ref[...] = (keep_ref[half:] + recv_ref[half:].astype(f32)).astype(bf16)


def halve_joined_body(keep_ref, recv_ref, rank_ref, rank_recv_ref, kept_ref, send_ref):
    half = keep_ref.shape[0] // 2
    kept_ref[:half] = keep_ref[:half] + recv_ref[:half].astype(f32)
    send_ref[:half] = (keep_ref[half:] + recv_ref[half:].astype(f32)).astype(bf16)
    rank = rank_ref[...] + rank_recv_ref[...]
    kept_ref[half:] = rank
    send_ref[half:] = rank.astype(bf16)


def halve_tail_body(keep_ref, recv_ref, kept_ref, send_ref):
    half = kept_ref.shape[0] - 2 * RANK
    kept_ref[:half] = keep_ref[:half] + recv_ref[:half].astype(f32)
    send_ref[:half] = (keep_ref[half : 2 * half] + recv_ref[half : 2 * half].astype(f32)).astype(bf16)
    total = keep_ref[2 * half :] + recv_ref[2 * half :].astype(f32)
    kept_ref[half:] = total
    send_ref[half:] = total.astype(bf16)


def halve(body, half, *args, **order):
    shape = (half, args[0].shape[1])
    return in_vmem(body, "halve", [(shape, f32), (shape, bf16)], *args, **order)


def hidden_body(
    gate_ref, gate_recv_ref, up_ref, up_recv_ref, gate_factor_ref, up_factor_ref, down_factor_ref, out_ref
):
    size = gate_factor_ref.shape[1]
    rank = (up_ref[size:] + up_recv_ref[size:].astype(f32)).astype(bf16)
    gate = lax.dot_general(
        gate_factor_ref[...], rank[:RANK], (((0,), (0,)), ((), ())), preferred_element_type=f32
    )
    gate = gate_ref[...] + gate_recv_ref[...].astype(f32) + adapter_scale * gate
    up = lax.dot_general(up_factor_ref[...], rank[RANK:], (((0,), (0,)), ((), ())), preferred_element_type=f32)
    up = up_ref[:size] + up_recv_ref[:size].astype(f32) + adapter_scale * up
    hidden = (gate / (1.0 + jnp.exp(-gate)) * up).astype(bf16)
    low = jnp.dot(down_factor_ref[...], hidden, preferred_element_type=f32).astype(bf16)
    for copy in range(out_ref.shape[0]):
        out_ref[copy, :size] = hidden
        out_ref[copy, size:] = low


def double_body(bit, mine_ref, theirs_ref, out_ref):
    count = mine_ref.shape[0]
    high = bit()
    out_ref[pl.ds(high * count, count)] = mine_ref[...]
    out_ref[pl.ds((1 - high) * count, count)] = theirs_ref[...]


def double_flat_body(bit, mine_ref, theirs_ref, out_ref):
    count, _, width = mine_ref.shape
    high = bit()
    for side, from_ref in ((high, mine_ref), (1 - high, theirs_ref)):
        for i in range(count):
            at = pl.multiple_of((side * count + i) * width, width)
            out_ref[:, pl.ds(at, width)] = from_ref[i]


def add_body(mine_ref, theirs_ref, out_ref):
    out_ref[...] = mine_ref[...] + theirs_ref[...]


def strip_body(from_ref, out_ref, low_ref):
    chips, size = from_ref.shape[0], from_ref.shape[1] - RANK
    low = jnp.zeros(low_ref.shape, f32)
    for chip in range(chips):
        out_ref[chip * size : (chip + 1) * size] = from_ref[chip, :size]
        low = low + from_ref[chip, size:].astype(f32)
    low_ref[...] = low


def down_rows_body(size, down_ref, own_ref, other_ref, token_ref, sem):
    core = lax.axis_index("c")
    token_ref[...] = jnp.zeros(token_ref.shape, f32)
    copies = []
    for side, to_ref in enumerate((own_ref, other_ref)):
        for chip in range(8):
            copies.append(
                pltpu.make_async_copy(
                    down_ref.at[rows_at(2 * chip + (core if side == 0 else 1 - core), size)],
                    to_ref.at[pl.ds(chip * size, size)],
                    sem.at[side * 8 + chip],
                )
            )
    for copy in copies:
        copy.start()
    for copy in copies:
        copy.wait()


def down_rows(size, down):
    units, width = down.shape
    half = jax.ShapeDtypeStruct((units // 2, width), down.dtype)
    whole = pl.BlockSpec(memory_space=pltpu.VMEM)
    return pl.pallas_call(
        functools.partial(down_rows_body, size),
        in_specs=[pl.BlockSpec(memory_space=pl.ANY)],
        out_specs=[whole] * 3,
        out_shape=[half, half, jax.ShapeDtypeStruct((8, 128), f32)],
        scratch_shapes=[pltpu.SemaphoreType.DMA((16,))],
        compiler_params=pltpu.CompilerParams(vmem_limit_bytes=VMEM_LIMIT),
        cost_estimate=pl.CostEstimate(flops=0, bytes_accessed=4 * units * width, transcendentals=0),
        name="down_rows",
    )(down)


def tp_blocks_body(own_ref, own_low_ref, other_ref, other_low_ref, factor_ref, out_ref):
    blocks, steps, block = out_ref.shape[:3]
    low = (own_low_ref[...] + other_low_ref[...]).astype(bf16)
    for s in range(steps):
        first = s * blocks * block
        rows = slice(first, first + blocks * block)
        term = lax.dot_general(
            low[:, rows], factor_ref[2 * RANK :], (((0,), (0,)), ((), ())), preferred_element_type=f32
        )
        total = (own_ref[rows] + other_ref[rows] + adapter_scale * term).astype(bf16)
        for t in range(blocks):
            out_ref[t, s] = total[t * block : (t + 1) * block]


def owner_sum_body(blocks_ref, out_ref):
    total = blocks_ref[0].astype(f32)
    for t in range(1, blocks_ref.shape[0]):
        total = total + blocks_ref[t].astype(f32)
    out_ref[...] = total.astype(bf16)


def per_device(
    normed,
    resident_gate_matrix,
    resident_up_matrix,
    resident_down_matrix,
    gate_input_factor,
    up_input_factor,
    gate_output_factor,
    up_output_factor,
    down_input_factor,
    down_output_factor,
):
    steps, rows, depth = normed.shape
    units = resident_gate_matrix.shape[1]
    size = units // 16
    lanes = steps * rows
    states = normed.reshape(lanes, depth)
    near, far, across = (
        functools.partial(ring_pair, "z", True),
        functools.partial(ring_pair, "z", False),
        functools.partial(swap, "yh"),
    )

    wide = jnp.concatenate([gate_input_factor, up_input_factor, down_output_factor.T], 0)[None]
    (wide,) = in_vmem(
        functools.partial(double_body, lambda: lax.axis_index("yl")),
        "double",
        [((2, *wide.shape[1:]), bf16)],
        wide,
        swap("yl", wide),
    )
    parts = [
        lax.dot_general(w, states, (((0,), (1,)), ((), ())), preferred_element_type=f32).astype(bf16)
        for w in (resident_gate_matrix, resident_up_matrix)
    ]
    recvs, sums, tokens = [], [], []
    for part, y_first in zip(parts, (True, False)):
        (send,) = in_vmem(
            functools.partial(other_core_body, size, y_first), "other_core", [((units // 2, lanes), bf16)], part
        )
        recvs.append(swap("c", send))
    for part, recv, y_first in zip(parts, recvs, (True, False)):
        shape = (4 * size, lanes)
        keep, send, token = in_vmem(
            functools.partial(core_sum_body, size, y_first),
            "core_sum",
            [(shape, f32), (shape, bf16)],
            part,
            recv,
            behind=tokens,
            token=True,
        )
        sums.append((keep, send))
        tokens = [token, wide]
    (wide,) = in_vmem(
        functools.partial(double_body, lambda: lax.axis_index("x") & 1),
        "double",
        [((4, *wide.shape[1:]), bf16)],
        wide,
        xor_pair("x", 1, wide),
    )
    (wide,) = in_vmem(
        functools.partial(double_flat_body, lambda: lax.axis_index("x") >> 1),
        "double",
        [((3 * RANK, depth), bf16)],
        wide,
        xor_pair("x", 3, wide),
    )
    rank = lax.dot_general(
        wide[: 2 * RANK], states, (((1,), (1,)), ((), ())), preferred_element_type=f32
    )
    (rank,) = in_vmem(add_body, "add", [(rank.shape, f32)], rank, swap("c", rank))

    *down, token = down_rows(size, resident_down_matrix)
    keep, send = sums[0]
    keep, send, crossed = halve(halve_body, 2 * size, keep, across(send), token=True)
    keep, send = halve(halve_body, size, keep, near(send))
    gate = keep, far(send)
    keep, send = sums[1]
    keep, send = halve(halve_joined_body, 2 * size + 2 * RANK, keep, near(send), rank, near(rank), behind=(crossed,))
    keep, send = halve(halve_tail_body, size + 2 * RANK, keep, far(send), behind=(token,))
    up = keep, across(send)
    (hidden,) = in_vmem(
        hidden_body,
        "hidden",
        [((8, size + RANK, lanes), bf16)],
        *gate,
        *up,
        gate_output_factor.T,
        up_output_factor.T,
        down_input_factor,
    )
    hidden = exchange(("yh", "z"), hidden)
    pieces = []
    for value, matrix in zip((hidden, swap("c", hidden)), down):
        value, low = in_vmem(
            strip_body, "strip", [((units // 2, lanes), bf16), ((RANK, lanes), f32)], value
        )
        part = lax.dot_general(value, matrix, (((0,), (0,)), ((), ())), preferred_element_type=f32)
        pieces += [part, low]
    (blocks,) = in_vmem(
        tp_blocks_body, "tp_blocks", [((8, steps, rows // 8, depth), bf16)], *pieces, wide
    )
    blocks = exchange(TP, blocks)
    return in_vmem(owner_sum_body, "owner_sum", [(blocks.shape[1:], bf16)], blocks)[0]


def solution(mesh):
    fine = Mesh(mesh.devices.reshape(2, 4, 2, 4, 2), FSDP + TP)
    fsdp, tp = FSDP, TP
    in_specs = (
        P(None, None, fsdp),
        P(fsdp, tp),
        P(fsdp, tp),
        P(tp, fsdp),
        P(None, fsdp + tp),
        P(None, fsdp + tp),
        P(tp + fsdp, None),
        P(tp + fsdp, None),
        P(None, tp + fsdp),
        P(fsdp + tp, None),
    )
    out_specs = P(None, tp, fsdp)
    return jax.shard_map(
        per_device, mesh=fine, in_specs=in_specs, out_specs=out_specs, check_vma=False
    )
```

```python
import functools

import jax
import jax.numpy as jnp
from jax import lax
from jax.experimental import pallas as pl
from jax.experimental.pallas import tpu as pltpu
from jax.sharding import Mesh
from jax.sharding import PartitionSpec as P

adapter_scale = 2.0
f32 = jnp.float32
bf16 = jnp.bfloat16
FSDP = ("yh", "z", "c")
TP = ("x", "yl")
RANK = 16
VMEM_LIMIT = 16 * 1024 * 1024


def pair_bits(core):
    return 1 + 2 * core, 3 - 2 * core


def owner(r, y_first):
    yh, z, c = lax.axis_index("yh"), lax.axis_index("z"), lax.axis_index("c")
    core, bits = (r >> 3) & 1, ((r >> 2) & 1, (r >> 1) & 1, r & 1)
    y, first_z, second_z = bits if y_first else (bits[2], bits[0], bits[1])
    cc = c ^ core
    a, b = pair_bits(cc)
    zz = z ^ (first_z * a) ^ (second_z * b)
    return ((yh ^ y) * 4 + zz) * 2 + cc


def swap(axis, value):
    return lax.ppermute(value, axis, [(0, 1), (1, 0)])


def ring_pair(axis, first, value):
    axes = ("z", "c") if axis == "z" else ("c", "x")

    def index(place, core):
        return place * 2 + core if axis == "z" else core * 4 + place

    moves = []
    for place in range(4):
        for core in range(2):
            step = pair_bits(core)[0 if first else 1]
            moves.append((index(place, core), index(place ^ step, core)))
    return lax.ppermute(value, axes, moves)


def xor_pair(axis, step, value):
    return lax.ppermute(value, axis, [(i, i ^ step) for i in range(4)])


def exchange(axes, value):
    return lax.all_to_all(value, axes, split_axis=0, concat_axis=0)


def in_vmem(body, name, out_shape, *args, behind=(), token=False):
    whole = pl.BlockSpec(memory_space=pltpu.VMEM)
    if token:
        out_shape = (*out_shape, ((8, 128), f32))
    outs = tuple(jax.ShapeDtypeStruct(shape, dtype) for shape, dtype in out_shape)
    moved = sum(a.size * a.dtype.itemsize for a in (*args, *outs))

    def kernel(*refs):
        out_refs = refs[len(args) + len(behind) :]
        if token:
            out_refs[-1][...] = jnp.zeros((8, 128), f32)
            out_refs = out_refs[:-1]
        body(*refs[: len(args)], *out_refs)

    return pl.pallas_call(
        kernel,
        in_specs=[whole] * (len(args) + len(behind)),
        out_specs=[whole] * len(outs),
        out_shape=outs,
        compiler_params=pltpu.CompilerParams(vmem_limit_bytes=VMEM_LIMIT),
        cost_estimate=pl.CostEstimate(flops=moved, bytes_accessed=moved, transcendentals=0),
        name=name,
    )(*args, *behind)


def rows_at(block, size):
    return pl.ds(pl.multiple_of(block * size, 16), size)


def other_core_body(size, y_first, part_ref, send_ref):
    for r in range(8):
        send_ref[r * size : (r + 1) * size] = part_ref[rows_at(owner(8 + r, y_first), size), :]


def core_sum_body(size, y_first, part_ref, recv_ref, keep_ref, send_ref):
    for r in range(8):
        at = r * size
        mine = rows_at(owner(r, y_first), size)
        total = part_ref[mine, :].astype(f32) + recv_ref[at : at + size].astype(f32)
        if r < 4:
            keep_ref[at : at + size] = total
        else:
            send_ref[at - 4 * size : at - 3 * size] = total.astype(bf16)


def halve_body(keep_ref, recv_ref, kept_ref, send_ref):
    half = kept_ref.shape[0]
    kept_ref[...] = keep_ref[:half] + recv_ref[:half].astype(f32)
    send_ref[...] = (keep_ref[half:] + recv_ref[half:].astype(f32)).astype(bf16)


def halve_joined_body(keep_ref, recv_ref, rank_ref, rank_recv_ref, kept_ref, send_ref):
    half = keep_ref.shape[0] // 2
    kept_ref[:half] = keep_ref[:half] + recv_ref[:half].astype(f32)
    send_ref[:half] = (keep_ref[half:] + recv_ref[half:].astype(f32)).astype(bf16)
    rank = rank_ref[...] + rank_recv_ref[...]
    kept_ref[half:] = rank
    send_ref[half:] = rank.astype(bf16)


def halve_tail_body(keep_ref, recv_ref, kept_ref, send_ref):
    half = kept_ref.shape[0] - 2 * RANK
    kept_ref[:half] = keep_ref[:half] + recv_ref[:half].astype(f32)
    send_ref[:half] = (keep_ref[half : 2 * half] + recv_ref[half : 2 * half].astype(f32)).astype(bf16)
    total = keep_ref[2 * half :] + recv_ref[2 * half :].astype(f32)
    kept_ref[half:] = total
    send_ref[half:] = total.astype(bf16)


def halve(body, half, *args, **order):
    shape = (half, args[0].shape[1])
    return in_vmem(body, "halve", [(shape, f32), (shape, bf16)], *args, **order)


def hidden_body(
    gate_ref, gate_recv_ref, up_ref, up_recv_ref, gate_factor_ref, up_factor_ref, down_factor_ref, out_ref
):
    size = gate_factor_ref.shape[1]
    rank = (up_ref[size:] + up_recv_ref[size:].astype(f32)).astype(bf16)
    gate = lax.dot_general(
        gate_factor_ref[...], rank[:RANK], (((0,), (0,)), ((), ())), preferred_element_type=f32
    )
    gate = gate_ref[...] + gate_recv_ref[...].astype(f32) + adapter_scale * gate
    up = lax.dot_general(up_factor_ref[...], rank[RANK:], (((0,), (0,)), ((), ())), preferred_element_type=f32)
    up = up_ref[:size] + up_recv_ref[:size].astype(f32) + adapter_scale * up
    hidden = (gate / (1.0 + jnp.exp(-gate)) * up).astype(bf16)
    low = jnp.dot(down_factor_ref[...], hidden, preferred_element_type=f32).astype(bf16)
    for copy in range(out_ref.shape[0]):
        out_ref[copy, :size] = hidden
        out_ref[copy, size:] = low


def double_body(bit, mine_ref, theirs_ref, out_ref):
    count = mine_ref.shape[0]
    high = bit()
    out_ref[pl.ds(high * count, count)] = mine_ref[...]
    out_ref[pl.ds((1 - high) * count, count)] = theirs_ref[...]


def double_flat_body(bit, mine_ref, theirs_ref, out_ref):
    count, _, width = mine_ref.shape
    high = bit()
    for side, from_ref in ((high, mine_ref), (1 - high, theirs_ref)):
        for i in range(count):
            at = pl.multiple_of((side * count + i) * width, width)
            out_ref[:, pl.ds(at, width)] = from_ref[i]


def add_body(mine_ref, theirs_ref, out_ref):
    out_ref[...] = mine_ref[...] + theirs_ref[...]


def strip_body(from_ref, out_ref, low_ref):
    chips, size = from_ref.shape[0], from_ref.shape[1] - RANK
    low = jnp.zeros(low_ref.shape, f32)
    for chip in range(chips):
        out_ref[chip * size : (chip + 1) * size] = from_ref[chip, :size]
        low = low + from_ref[chip, size:].astype(f32)
    low_ref[...] = low


def down_rows_body(size, down_ref, own_ref, other_ref, token_ref, sem):
    core = lax.axis_index("c")
    token_ref[...] = jnp.zeros(token_ref.shape, f32)
    copies = []
    for side, to_ref in enumerate((own_ref, other_ref)):
        for chip in range(8):
            copies.append(
                pltpu.make_async_copy(
                    down_ref.at[rows_at(2 * chip + (core if side == 0 else 1 - core), size)],
                    to_ref.at[pl.ds(chip * size, size)],
                    sem.at[side * 8 + chip],
                )
            )
    for copy in copies:
        copy.start()
    for copy in copies:
        copy.wait()


def down_rows(size, down):
    units, width = down.shape
    half = jax.ShapeDtypeStruct((units // 2, width), down.dtype)
    whole = pl.BlockSpec(memory_space=pltpu.VMEM)
    return pl.pallas_call(
        functools.partial(down_rows_body, size),
        in_specs=[pl.BlockSpec(memory_space=pl.ANY)],
        out_specs=[whole] * 3,
        out_shape=[half, half, jax.ShapeDtypeStruct((8, 128), f32)],
        scratch_shapes=[pltpu.SemaphoreType.DMA((16,))],
        compiler_params=pltpu.CompilerParams(vmem_limit_bytes=VMEM_LIMIT),
        cost_estimate=pl.CostEstimate(flops=0, bytes_accessed=4 * units * width, transcendentals=0),
        name="down_rows",
    )(down)


def tp_blocks_body(own_ref, own_low_ref, other_ref, other_low_ref, factor_ref, out_ref):
    blocks, steps, block = out_ref.shape[:3]
    low = (own_low_ref[...] + other_low_ref[...]).astype(bf16)
    for s in range(steps):
        first = s * blocks * block
        rows = slice(first, first + blocks * block)
        term = lax.dot_general(
            low[:, rows], factor_ref[2 * RANK :], (((0,), (0,)), ((), ())), preferred_element_type=f32
        )
        total = (own_ref[rows] + other_ref[rows] + adapter_scale * term).astype(bf16)
        for t in range(blocks):
            out_ref[t, s] = total[t * block : (t + 1) * block]


def owner_sum_body(blocks_ref, out_ref):
    total = blocks_ref[0].astype(f32)
    for t in range(1, blocks_ref.shape[0]):
        total = total + blocks_ref[t].astype(f32)
    out_ref[...] = total.astype(bf16)


def per_device(
    normed,
    resident_gate_matrix,
    resident_up_matrix,
    resident_down_matrix,
    gate_input_factor,
    up_input_factor,
    gate_output_factor,
    up_output_factor,
    down_input_factor,
    down_output_factor,
):
    steps, rows, depth = normed.shape
    units = resident_gate_matrix.shape[1]
    size = units // 16
    lanes = steps * rows
    states = normed.reshape(lanes, depth)
    near, far, across = (
        functools.partial(ring_pair, "z", True),
        functools.partial(ring_pair, "z", False),
        functools.partial(swap, "yh"),
    )

    wide = jnp.concatenate([gate_input_factor, up_input_factor, down_output_factor.T], 0)[None]
    (wide,) = in_vmem(
        functools.partial(double_body, lambda: lax.axis_index("yl")),
        "double",
        [((2, *wide.shape[1:]), bf16)],
        wide,
        swap("yl", wide),
    )
    parts = [
        lax.dot_general(w, states, (((0,), (1,)), ((), ())), preferred_element_type=f32).astype(bf16)
        for w in (resident_gate_matrix, resident_up_matrix)
    ]
    recvs, sums, tokens = [], [], []
    for part, y_first in zip(parts, (True, False)):
        (send,) = in_vmem(
            functools.partial(other_core_body, size, y_first), "other_core", [((units // 2, lanes), bf16)], part, behind=() if y_first else (wide,)
        )
        recvs.append(swap("c", send))
    for part, recv, y_first in zip(parts, recvs, (True, False)):
        shape = (4 * size, lanes)
        keep, send, token = in_vmem(
            functools.partial(core_sum_body, size, y_first),
            "core_sum",
            [(shape, f32), (shape, bf16)],
            part,
            recv,
            behind=tokens,
            token=True,
        )
        sums.append((keep, send))
        tokens = [token, wide]
    (wide,) = in_vmem(
        functools.partial(double_body, lambda: lax.axis_index("x") & 1),
        "double",
        [((4, *wide.shape[1:]), bf16)],
        wide,
        xor_pair("x", 1, wide),
    )
    (wide,) = in_vmem(
        functools.partial(double_flat_body, lambda: lax.axis_index("x") >> 1),
        "double",
        [((3 * RANK, depth), bf16)],
        wide,
        xor_pair("x", 3, wide),
    )
    rank = lax.dot_general(
        wide[: 2 * RANK], states, (((1,), (1,)), ((), ())), preferred_element_type=f32
    )
    (rank,) = in_vmem(add_body, "add", [(rank.shape, f32)], rank, swap("c", rank))

    *down, token = down_rows(size, resident_down_matrix)
    keep, send = sums[0]
    keep, send, crossed = halve(halve_body, 2 * size, keep, across(send), token=True)
    keep, send = halve(halve_body, size, keep, near(send))
    gate = keep, far(send)
    keep, send = sums[1]
    keep, send = halve(halve_joined_body, 2 * size + 2 * RANK, keep, near(send), rank, near(rank), behind=(crossed,))
    keep, send = halve(halve_tail_body, size + 2 * RANK, keep, far(send), behind=(token,))
    up = keep, across(send)
    (hidden,) = in_vmem(
        hidden_body,
        "hidden",
        [((8, size + RANK, lanes), bf16)],
        *gate,
        *up,
        gate_output_factor.T,
        up_output_factor.T,
        down_input_factor,
    )
    hidden = exchange(("yh", "z"), hidden)
    pieces = []
    for value, matrix in zip((hidden, swap("c", hidden)), down):
        value, low = in_vmem(
            strip_body, "strip", [((units // 2, lanes), bf16), ((RANK, lanes), f32)], value
        )
        part = lax.dot_general(value, matrix, (((0,), (0,)), ((), ())), preferred_element_type=f32)
        pieces += [part, low]
    (blocks,) = in_vmem(
        tp_blocks_body, "tp_blocks", [((8, steps, rows // 8, depth), bf16)], *pieces, wide
    )
    blocks = exchange(TP, blocks)
    return in_vmem(owner_sum_body, "owner_sum", [(blocks.shape[1:], bf16)], blocks)[0]


def solution(mesh):
    fine = Mesh(mesh.devices.reshape(2, 4, 2, 4, 2), FSDP + TP)
    fsdp, tp = FSDP, TP
    in_specs = (
        P(None, None, fsdp),
        P(fsdp, tp),
        P(fsdp, tp),
        P(tp, fsdp),
        P(None, fsdp + tp),
        P(None, fsdp + tp),
        P(tp + fsdp, None),
        P(tp + fsdp, None),
        P(None, tp + fsdp),
        P(fsdp + tp, None),
    )
    out_specs = P(None, tp, fsdp)
    return jax.shard_map(
        per_device, mesh=fine, in_specs=in_specs, out_specs=out_specs, check_vma=False
    )
```

```python
import functools

import jax
import jax.numpy as jnp
from jax import lax
from jax.experimental import pallas as pl
from jax.experimental.pallas import tpu as pltpu
from jax.sharding import Mesh
from jax.sharding import PartitionSpec as P

adapter_scale = 2.0
f32 = jnp.float32
bf16 = jnp.bfloat16
FSDP = ("yh", "z", "c")
TP = ("x", "yl")
RANK = 16
VMEM_LIMIT = 12 * 1024 * 1024


def pair_bits(core):
    return 1 + 2 * core, 3 - 2 * core


def owner(r, y_first):
    yh, z, c = lax.axis_index("yh"), lax.axis_index("z"), lax.axis_index("c")
    core, bits = (r >> 3) & 1, ((r >> 2) & 1, (r >> 1) & 1, r & 1)
    y, first_z, second_z = bits if y_first else (bits[2], bits[0], bits[1])
    cc = c ^ core
    a, b = pair_bits(cc)
    zz = z ^ (first_z * a) ^ (second_z * b)
    return ((yh ^ y) * 4 + zz) * 2 + cc


def swap(axis, value):
    return lax.ppermute(value, axis, [(0, 1), (1, 0)])


def ring_pair(axis, first, value):
    axes = ("z", "c") if axis == "z" else ("c", "x")

    def index(place, core):
        return place * 2 + core if axis == "z" else core * 4 + place

    moves = []
    for place in range(4):
        for core in range(2):
            step = pair_bits(core)[0 if first else 1]
            moves.append((index(place, core), index(place ^ step, core)))
    return lax.ppermute(value, axes, moves)


def xor_pair(axis, step, value):
    return lax.ppermute(value, axis, [(i, i ^ step) for i in range(4)])


def exchange(axes, value):
    return lax.all_to_all(value, axes, split_axis=0, concat_axis=0)


def in_vmem(body, name, out_shape, *args, behind=(), token=False):
    whole = pl.BlockSpec(memory_space=pltpu.VMEM)
    if token:
        out_shape = (*out_shape, ((8, 128), f32))
    outs = tuple(jax.ShapeDtypeStruct(shape, dtype) for shape, dtype in out_shape)
    moved = sum(a.size * a.dtype.itemsize for a in (*args, *outs))

    def kernel(*refs):
        out_refs = refs[len(args) + len(behind) :]
        if token:
            out_refs[-1][...] = jnp.zeros((8, 128), f32)
            out_refs = out_refs[:-1]
        body(*refs[: len(args)], *out_refs)

    return pl.pallas_call(
        kernel,
        in_specs=[whole] * (len(args) + len(behind)),
        out_specs=[whole] * len(outs),
        out_shape=outs,
        compiler_params=pltpu.CompilerParams(vmem_limit_bytes=VMEM_LIMIT),
        cost_estimate=pl.CostEstimate(flops=moved, bytes_accessed=moved, transcendentals=0),
        name=name,
    )(*args, *behind)


def rows_at(block, size):
    return pl.ds(pl.multiple_of(block * size, 16), size)


def other_core_body(size, y_first, part_ref, send_ref):
    for r in range(8):
        send_ref[r * size : (r + 1) * size] = part_ref[rows_at(owner(8 + r, y_first), size), :]


def core_sum_body(size, y_first, part_ref, recv_ref, keep_ref, send_ref):
    for r in range(8):
        at = r * size
        mine = rows_at(owner(r, y_first), size)
        total = part_ref[mine, :].astype(f32) + recv_ref[at : at + size].astype(f32)
        if r < 4:
            keep_ref[at : at + size] = total
        else:
            send_ref[at - 4 * size : at - 3 * size] = total.astype(bf16)


def halve_body(keep_ref, recv_ref, kept_ref, send_ref):
    half = kept_ref.shape[0]
    kept_ref[...] = keep_ref[:half] + recv_ref[:half].astype(f32)
    send_ref[...] = (keep_ref[half:] + recv_ref[half:].astype(f32)).astype(bf16)


def halve_joined_body(keep_ref, recv_ref, rank_ref, rank_recv_ref, kept_ref, send_ref):
    half = keep_ref.shape[0] // 2
    kept_ref[:half] = keep_ref[:half] + recv_ref[:half].astype(f32)
    send_ref[:half] = (keep_ref[half:] + recv_ref[half:].astype(f32)).astype(bf16)
    rank = rank_ref[...] + rank_recv_ref[...]
    kept_ref[half:] = rank
    send_ref[half:] = rank.astype(bf16)


def halve_tail_body(keep_ref, recv_ref, kept_ref, send_ref):
    half = kept_ref.shape[0] - 2 * RANK
    kept_ref[:half] = keep_ref[:half] + recv_ref[:half].astype(f32)
    send_ref[:half] = (keep_ref[half : 2 * half] + recv_ref[half : 2 * half].astype(f32)).astype(bf16)
    total = keep_ref[2 * half :] + recv_ref[2 * half :].astype(f32)
    kept_ref[half:] = total
    send_ref[half:] = total.astype(bf16)


def halve(body, half, *args, **order):
    shape = (half, args[0].shape[1])
    return in_vmem(body, "halve", [(shape, f32), (shape, bf16)], *args, **order)


def hidden_body(
    gate_ref, gate_recv_ref, up_ref, up_recv_ref, gate_factor_ref, up_factor_ref, down_factor_ref, out_ref
):
    size = gate_factor_ref.shape[1]
    rank = (up_ref[size:] + up_recv_ref[size:].astype(f32)).astype(bf16)
    gate = lax.dot_general(
        gate_factor_ref[...], rank[:RANK], (((0,), (0,)), ((), ())), preferred_element_type=f32
    )
    gate = gate_ref[...] + gate_recv_ref[...].astype(f32) + adapter_scale * gate
    up = lax.dot_general(up_factor_ref[...], rank[RANK:], (((0,), (0,)), ((), ())), preferred_element_type=f32)
    up = up_ref[:size] + up_recv_ref[:size].astype(f32) + adapter_scale * up
    hidden = (gate / (1.0 + jnp.exp(-gate)) * up).astype(bf16)
    low = jnp.dot(down_factor_ref[...], hidden, preferred_element_type=f32).astype(bf16)
    for copy in range(out_ref.shape[0]):
        out_ref[copy, :size] = hidden
        out_ref[copy, size:] = low


def double_body(bit, mine_ref, theirs_ref, out_ref):
    count = mine_ref.shape[0]
    high = bit()
    out_ref[pl.ds(high * count, count)] = mine_ref[...]
    out_ref[pl.ds((1 - high) * count, count)] = theirs_ref[...]


def double_flat_body(bit, mine_ref, theirs_ref, out_ref):
    count, _, width = mine_ref.shape
    high = bit()
    for side, from_ref in ((high, mine_ref), (1 - high, theirs_ref)):
        for i in range(count):
            at = pl.multiple_of((side * count + i) * width, width)
            out_ref[:, pl.ds(at, width)] = from_ref[i]


def add_body(mine_ref, theirs_ref, out_ref):
    out_ref[...] = mine_ref[...] + theirs_ref[...]


def strip_body(from_ref, out_ref, low_ref):
    chips, size = from_ref.shape[0], from_ref.shape[1] - RANK
    low = jnp.zeros(low_ref.shape, f32)
    for chip in range(chips):
        out_ref[chip * size : (chip + 1) * size] = from_ref[chip, :size]
        low = low + from_ref[chip, size:].astype(f32)
    low_ref[...] = low


def down_rows_body(size, down_ref, own_ref, other_ref, token_ref, sem):
    core = lax.axis_index("c")
    token_ref[...] = jnp.zeros(token_ref.shape, f32)
    copies = []
    for side, to_ref in enumerate((own_ref, other_ref)):
        for chip in range(8):
            copies.append(
                pltpu.make_async_copy(
                    down_ref.at[rows_at(2 * chip + (core if side == 0 else 1 - core), size)],
                    to_ref.at[pl.ds(chip * size, size)],
                    sem.at[side * 8 + chip],
                )
            )
    for copy in copies:
        copy.start()
    for copy in copies:
        copy.wait()


def down_rows(size, down):
    units, width = down.shape
    half = jax.ShapeDtypeStruct((units // 2, width), down.dtype)
    whole = pl.BlockSpec(memory_space=pltpu.VMEM)
    return pl.pallas_call(
        functools.partial(down_rows_body, size),
        in_specs=[pl.BlockSpec(memory_space=pl.ANY)],
        out_specs=[whole] * 3,
        out_shape=[half, half, jax.ShapeDtypeStruct((8, 128), f32)],
        scratch_shapes=[pltpu.SemaphoreType.DMA((16,))],
        compiler_params=pltpu.CompilerParams(vmem_limit_bytes=VMEM_LIMIT),
        cost_estimate=pl.CostEstimate(flops=0, bytes_accessed=4 * units * width, transcendentals=0),
        name="down_rows",
    )(down)


def tp_blocks_body(own_ref, own_low_ref, other_ref, other_low_ref, factor_ref, out_ref):
    blocks, steps, block = out_ref.shape[:3]
    low = (own_low_ref[...] + other_low_ref[...]).astype(bf16)
    for s in range(steps):
        first = s * blocks * block
        rows = slice(first, first + blocks * block)
        term = lax.dot_general(
            low[:, rows], factor_ref[2 * RANK :], (((0,), (0,)), ((), ())), preferred_element_type=f32
        )
        total = (own_ref[rows] + other_ref[rows] + adapter_scale * term).astype(bf16)
        for t in range(blocks):
            out_ref[t, s] = total[t * block : (t + 1) * block]


def owner_sum_body(blocks_ref, out_ref):
    total = blocks_ref[0].astype(f32)
    for t in range(1, blocks_ref.shape[0]):
        total = total + blocks_ref[t].astype(f32)
    out_ref[...] = total.astype(bf16)


def per_device(
    normed,
    resident_gate_matrix,
    resident_up_matrix,
    resident_down_matrix,
    gate_input_factor,
    up_input_factor,
    gate_output_factor,
    up_output_factor,
    down_input_factor,
    down_output_factor,
):
    steps, rows, depth = normed.shape
    units = resident_gate_matrix.shape[1]
    size = units // 16
    lanes = steps * rows
    states = normed.reshape(lanes, depth)
    near, far, across = (
        functools.partial(ring_pair, "z", True),
        functools.partial(ring_pair, "z", False),
        functools.partial(swap, "yh"),
    )

    wide = jnp.concatenate([gate_input_factor, up_input_factor, down_output_factor.T], 0)[None]
    (wide,) = in_vmem(
        functools.partial(double_body, lambda: lax.axis_index("yl")),
        "double",
        [((2, *wide.shape[1:]), bf16)],
        wide,
        swap("yl", wide),
    )
    parts = [
        lax.dot_general(w, states, (((0,), (1,)), ((), ())), preferred_element_type=f32).astype(bf16)
        for w in (resident_gate_matrix, resident_up_matrix)
    ]
    recvs, sums, tokens = [], [], []
    for part, y_first in zip(parts, (True, False)):
        (send,) = in_vmem(
            functools.partial(other_core_body, size, y_first), "other_core", [((units // 2, lanes), bf16)], part, behind=() if y_first else (wide,)
        )
        recvs.append(swap("c", send))
    for part, recv, y_first in zip(parts, recvs, (True, False)):
        shape = (4 * size, lanes)
        keep, send, token = in_vmem(
            functools.partial(core_sum_body, size, y_first),
            "core_sum",
            [(shape, f32), (shape, bf16)],
            part,
            recv,
            behind=tokens,
            token=True,
        )
        sums.append((keep, send))
        tokens = [token, wide]
    (wide,) = in_vmem(
        functools.partial(double_body, lambda: lax.axis_index("x") & 1),
        "double",
        [((4, *wide.shape[1:]), bf16)],
        wide,
        xor_pair("x", 1, wide),
    )
    (wide,) = in_vmem(
        functools.partial(double_flat_body, lambda: lax.axis_index("x") >> 1),
        "double",
        [((3 * RANK, depth), bf16)],
        wide,
        xor_pair("x", 3, wide),
    )
    rank = lax.dot_general(
        wide[: 2 * RANK], states, (((1,), (1,)), ((), ())), preferred_element_type=f32
    )
    (rank,) = in_vmem(add_body, "add", [(rank.shape, f32)], rank, swap("c", rank))

    *down, token = down_rows(size, resident_down_matrix)
    keep, send = sums[0]
    keep, send, crossed = halve(halve_body, 2 * size, keep, across(send), token=True)
    keep, send = halve(halve_body, size, keep, near(send))
    gate = keep, far(send)
    keep, send = sums[1]
    keep, send = halve(halve_joined_body, 2 * size + 2 * RANK, keep, near(send), rank, near(rank), behind=(crossed,))
    keep, send = halve(halve_tail_body, size + 2 * RANK, keep, far(send), behind=(token,))
    up = keep, across(send)
    (hidden,) = in_vmem(
        hidden_body,
        "hidden",
        [((8, size + RANK, lanes), bf16)],
        *gate,
        *up,
        gate_output_factor.T,
        up_output_factor.T,
        down_input_factor,
    )
    hidden = exchange(("yh", "z"), hidden)
    pieces = []
    for value, matrix in zip((hidden, swap("c", hidden)), down):
        value, low = in_vmem(
            strip_body, "strip", [((units // 2, lanes), bf16), ((RANK, lanes), f32)], value
        )
        part = lax.dot_general(value, matrix, (((0,), (0,)), ((), ())), preferred_element_type=f32)
        pieces += [part, low]
    (blocks,) = in_vmem(
        tp_blocks_body, "tp_blocks", [((8, steps, rows // 8, depth), bf16)], *pieces, wide
    )
    blocks = exchange(TP, blocks)
    return in_vmem(owner_sum_body, "owner_sum", [(blocks.shape[1:], bf16)], blocks)[0]


def solution(mesh):
    fine = Mesh(mesh.devices.reshape(2, 4, 2, 4, 2), FSDP + TP)
    fsdp, tp = FSDP, TP
    in_specs = (
        P(None, None, fsdp),
        P(fsdp, tp),
        P(fsdp, tp),
        P(tp, fsdp),
        P(None, fsdp + tp),
        P(None, fsdp + tp),
        P(tp + fsdp, None),
        P(tp + fsdp, None),
        P(None, tp + fsdp),
        P(fsdp + tp, None),
    )
    out_specs = P(None, tp, fsdp)
    return jax.shard_map(
        per_device, mesh=fine, in_specs=in_specs, out_specs=out_specs, check_vma=False
    )
```
